32 devices in a mesh: lat: 4 (over x, core), lon: 8 (over z, y).
Axes of the slice: x: 2, y: 2, z: 4, core: 2. Of those that a mesh axis runs over, the one named last changes fastest.
Arguments:
- control: float32 [80, 128, 1024], P(None, 'lat', 'lon'), may hold values from -6 to 6
- vertical: float32 [80, 80], replicated, may hold values from -0.625 to 0.625
- kappa: float32 [128, 1024], P('lat', 'lon'), may hold values from 0.03 to 0.24
- obs_weights: bfloat16 [80, 131072], P(None, ('lat', 'lon')), may hold values from -0.625 to 0.625
- obs_values: bfloat16 [131072], P(('lat', 'lon')), may hold values from -6 to 6
- obs_precision: bfloat16 [131072], P(('lat', 'lon')), may hold values from 0.5 to 4
- obs_slot: int32 [131072], P(('lat', 'lon')), may hold values from 0 to 8191, as said below
- obs_column: int32 [131072], P(('lat', 'lon')), may hold values from 0 to 4095
Outputs:
- gradient: float32 [80, 128, 1024], P(None, 'lat', 'lon')
The draws below stay inside these ranges and needn't reach their ends.
Inputs may be any that keep to these rules, and one draw needn't show every extreme that they name: `obs_slot`: on each device the slots of its observations are distinct; slot // 256 is the owning device, numbered with the lat index slowest. At most 256 observations of one device go to one owner, and some owner receives exactly 256 from every device.
All inputs are finite; a program needn't handle non-finite values.
Results may differ from the reference program's by a relative error of at most 0.00035.
Values may be sent and summed in bfloat16 or wider, within the bound.
A program may use at most 64 MiB of HBM per device.

```python
import math
import jax
import jax.numpy as jnp
from jax import lax

K = 80
CLAT = 32
CLON = 128
NSTEP = 4
OBS_DEV = 4096
CAP = 256
OBSERVATIONS = 131072
NLAT = 128
NLON = 1024
N_LON = 8
DEVICES = 32


def draw_obs_slot(key, part):
    total_slot_count = DEVICES * CAP
    key_rank, key_jitter, key_order = jax.random.split(jax.random.fold_in(key, 7), 3)
    position = jax.random.permutation(key_rank, DEVICES)
    target_level_group = position * 4 // DEVICES
    heaviest_loaded = (position == DEVICES - 1).astype(jnp.int32)
    vertical_level_boost = target_level_group * 256 + heaviest_loaded * 8192
    target_index = jnp.arange(total_slot_count) // CAP
    random_perturbation = jax.random.randint(key_jitter, (DEVICES, total_slot_count), 0, 1024)
    routing_scores = (vertical_level_boost[target_index][None, :] + random_perturbation) * total_slot_count + jnp.arange(total_slot_count)[None, :]
    unused, chosen = lax.top_k(routing_scores, OBS_DEV)
    chosen = jax.random.permutation(key_order, chosen, axis=1, independent=True)
    return chosen.reshape(-1).astype(jnp.int32)


def place_ends(entries, rng, least, top_value):
    extent = entries.shape
    place = [jax.random.randint(jax.random.fold_in(rng, axis), (), 0, extent[axis]) for axis in range(len(extent))]
    entries = entries.at[tuple(place)].set(least)
    longest = extent.index(max(extent))
    place[longest] = (place[longest] + 1) % extent[longest]
    return entries.at[tuple(place)].set(top_value)


def block_levels(rng, dims, cuts, smallest, high):
    factor_of, own = 1.0, jax.random.fold_in(rng, 6)
    for dim, blocks in cuts:
        heights = jnp.exp(jax.random.uniform(jax.random.fold_in(own, dim), (blocks,), jnp.float32, smallest / len(cuts), high / len(cuts)))
        factor_of = factor_of * jnp.repeat(heights, dims[dim] // blocks).reshape([-1 if axis == dim else 1 for axis in range(len(dims))])
    return factor_of


def noise(key, dims, scale, bound, cuts=(), dtype=jnp.bfloat16):
    gain = block_levels(key, dims, cuts, -0.22, 0.18) if cuts else 1.0
    values = jax.random.normal(key, dims, jnp.float32) * scale * gain
    return jnp.minimum(jnp.maximum(values, -bound), bound).astype(dtype)


def setup_inputs(seed: int = 0) -> dict:
    seeds = jax.random.split(jax.random.key(seed), 9)
    return {
        "control": noise(seeds[0], (K, NLAT, NLON), 1.0, 6.0, ((1, 4), (2, 8)), jnp.float32),
        "vertical": noise(seeds[1], (K, K), K ** -0.5, 0.625, (), jnp.float32),
        "kappa": jnp.clip(jnp.exp(math.log(0.24) - 2.0794415 * jax.random.uniform(seeds[2], (NLAT, NLON), jnp.float32) ** block_levels(seeds[2], (NLAT, NLON), ((0, 4), (1, 8)), -0.2, 0.2)), 0.03, 0.24),
        "obs_weights": noise(seeds[3], (K, OBSERVATIONS), K ** -0.5, 0.625, ((1, 32),)),
        "obs_values": noise(seeds[4], (OBSERVATIONS,), 1.0, 6.0, ((0, 32),)),
        "obs_precision": jnp.clip(jnp.exp(math.log(4.0) - 2.0794415 * jax.random.uniform(seeds[5], (OBSERVATIONS,), jnp.float32) ** block_levels(seeds[5], (OBSERVATIONS,), ((0, 32),), -0.2, 0.2)), 0.5, 4.0).astype(jnp.bfloat16),
        "obs_slot": draw_obs_slot(jax.random.fold_in(seeds[8], 71), 0),
        "obs_column": place_ends(jax.random.randint(seeds[7], (OBSERVATIONS,), 0, CLAT * CLON), jax.random.fold_in(seeds[7], 1), 0, (CLAT * CLON) - 1).astype(jnp.int32),
    }


def laplace(field):
    padded = jnp.pad(field, ((0, 0), (1, 1), (0, 0)))
    north_south = padded[:, :-2, :] + padded[:, 2:, :]
    east_west = jnp.roll(field, -1, axis=2) + jnp.roll(field, 1, axis=2)
    return north_south + east_west - 4.0 * field


def reference(control, vertical, kappa, obs_weights, obs_values, obs_precision, obs_slot, obs_column):
    increment = jnp.einsum("kj,jab->kab", vertical, control, precision=lax.Precision.HIGHEST)
    for step_index in range(NSTEP):
        increment = increment + kappa * laplace(increment)
    owner_dev = obs_slot // CAP
    lat_global = (owner_dev // N_LON) * CLAT + obs_column // CLON
    lon_global = (owner_dev % N_LON) * CLON + obs_column % CLON
    flat_index = (lat_global * NLON + lon_global).astype(jnp.int32)
    flat_state = increment.reshape(K, NLAT * NLON)
    picked = jnp.take(flat_state, flat_index, axis=1)
    weights_f = obs_weights.astype(jnp.float32)
    model_obs = jnp.sum(weights_f * picked, axis=0)
    weighted = obs_precision.astype(jnp.float32) * (obs_values.astype(jnp.float32) - model_obs)
    adjoint_flat = jnp.zeros((K, NLAT * NLON), jnp.float32).at[:, flat_index].add(weights_f * weighted[None, :])
    adjoint_field = -adjoint_flat.reshape(K, NLAT, NLON)
    for step_index in range(NSTEP):
        adjoint_field = adjoint_field + laplace(kappa * adjoint_field)
    back = jnp.einsum("jk,jab->kab", vertical, adjoint_field, precision=lax.Precision.HIGHEST)
    return control + back
```

```python
import functools

import jax
import jax.numpy as jnp
from jax import lax
from jax.experimental import pallas as pl
from jax.experimental.pallas import tpu as pltpu
from jax.sharding import PartitionSpec as P

NSTEP = 4
LANES = 128
CHAINS = 8
VMEM = pl.BlockSpec(memory_space=pltpu.VMEM)
SMEM = pl.BlockSpec(memory_space=pltpu.SMEM)
PARAMS = pltpu.CompilerParams(vmem_limit_bytes=56 * 2**20)


def pack_kernel(slot_ref, payload_ref, out_ref, rows, slots):
    obs = rows.shape[0]

    @pl.loop(0, obs // LANES)
    def _(j):
        at = pl.multiple_of(j * LANES, LANES)
        rows[pl.ds(at, LANES), :] = payload_ref[:, pl.ds(at, LANES)].T

    @pl.loop(0, slots.shape[0] // 256)
    def _(j):
        at = pl.multiple_of(j * 256, 256)
        slots[pl.ds(at, 256), :] = jnp.zeros((256, LANES), jnp.float32)

    @pl.loop(0, obs // 32)
    def _(j):
        at = pl.multiple_of(j * 32, 32)
        for u in range(32):
            slots[pl.ds(slot_ref[at + u], 1), :] = rows[pl.ds(at + u, 1), :]

    @pl.loop(0, slots.shape[0] // 256)
    def _(j):
        at = pl.multiple_of(j * 256, 256)
        out_ref[pl.ds(at, 256), :] = slots[pl.ds(at, 256), :].astype(jnp.bfloat16)


def obs_kernel(levels, col_ref, got_ref, state_ref, out_ref, picked, *sums):
    count = picked.shape[0]
    cells = state_ref.shape[0]

    @pl.loop(0, cells // 256)
    def _(j):
        at = pl.multiple_of(j * 256, 256)
        for s in sums:
            s[pl.ds(at, 256), :] = jnp.zeros((256, LANES), jnp.float32)

    @pl.loop(0, count // 32)
    def _(j):
        at = pl.multiple_of(j * 32, 32)
        for u in range(32):
            picked[pl.ds(at + u, 1), :] = state_ref[pl.ds(col_ref[at + u], 1), :]

    @pl.loop(0, count // 128)
    def _(j):
        at = pl.multiple_of(j * 128, 128)
        w = got_ref[pl.ds(at, 128), :].astype(jnp.float32)
        model = jnp.sum(w * picked[pl.ds(at, 128), :], axis=1, keepdims=True)
        weighted = w[:, levels + 1 : levels + 2] * (model - w[:, levels : levels + 1])
        picked[pl.ds(at, 128), :] = w * weighted

    @pl.loop(0, count // 32)
    def _(j):
        at = pl.multiple_of(j * 32, 32)
        for u in range(0, 32, CHAINS):
            cols = [col_ref[at + u + c] for c in range(CHAINS)]
            old = [sums[c][pl.ds(cols[c], 1), :] for c in range(CHAINS)]
            for c in range(CHAINS):
                sums[c][pl.ds(cols[c], 1), :] = old[c] + picked[pl.ds(at + u + c, 1), :]

    @pl.loop(0, cells // 64)
    def _(j):
        at = pl.multiple_of(j * 64, 64)
        parts = [s[pl.ds(at, 64), :] for s in sums]
        while len(parts) > 1:
            parts = [a + b for a, b in zip(parts[::2], parts[1::2])]
        out_ref[pl.ds(at, 64), :] = parts[0]


def ring(row):
    width = row.shape[0]
    return pltpu.roll(row, 1, 0) + pltpu.roll(row, width - 1, 0)


def forward_kernel(field_ref, kappa_ref, out_ref, one, two):
    rows, lon = out_ref.shape[:2]
    total = field_ref.shape[0]
    source = field_ref
    for step in range(NSTEP):
        last = step == NSTEP - 1
        target = (one, two)[step % 2]

        @pl.loop(1 + step, total - 1 - step)
        def _(r):
            f = source[r]
            new = f + kappa_ref[r] * (source[r - 1] + source[r + 1] + ring(f) - 4.0 * f)
            if last:
                out_ref[r - NSTEP] = new[:lon]
            else:
                target[r] = new

        source = target


def adjoint_kernel(field_ref, kappa_ref, out_ref, z, y):
    rows, lon = out_ref.shape[:2]
    total = field_ref.shape[0]
    source = field_ref
    for step in range(NSTEP):
        last = step == NSTEP - 1

        @pl.loop(step, total - step)
        def _(r):
            y[r] = kappa_ref[r] * source[r]

        @pl.loop(1 + step, total - 1 - step)
        def _(r):
            f = y[r]
            new = source[r] + (y[r - 1] + y[r + 1] + ring(f) - 4.0 * f)
            if last:
                out_ref[r - NSTEP] = new[:lon]
            else:
                z[r] = new

        source = z


def exchange(block, axis, dim, periodic, dtype):
    count = lax.axis_size(axis)
    forward = [(i, i + 1) for i in range(count - 1)]
    if periodic:
        forward.append((count - 1, 0))
    backward = [(target, source) for source, target in forward]
    size = block.shape[dim]
    low = lax.slice_in_dim(block, size - NSTEP, None, axis=dim).astype(dtype)
    high = lax.slice_in_dim(block, 0, NSTEP, axis=dim).astype(dtype)
    low = lax.ppermute(low, axis, forward).astype(block.dtype)
    high = lax.ppermute(high, axis, backward).astype(block.dtype)
    return low, high


def extended(block, dtype):
    low, high = exchange(block, "lon", 1, True, dtype)
    block = jnp.concatenate([block, high, low], axis=1)
    low, high = exchange(block, "lat", 0, False, dtype)
    return jnp.concatenate([low, block, high], axis=0)


def local(control, vertical, kappa, obs_weights, obs_values, obs_precision, obs_slot, obs_column):
    levels, lat_rows, lon_cells = control.shape
    devices = lax.axis_size("lat") * lax.axis_size("lon")
    obs_here = obs_slot.shape[0]
    slot_count = 2 * obs_here // devices
    total = devices * slot_count
    cells = lat_rows * lon_cells
    f32 = jnp.float32

    payload = jnp.concatenate(
        [
            obs_weights.astype(f32),
            obs_values.astype(f32)[None],
            obs_precision.astype(f32)[None],
            (obs_column // lon_cells).astype(f32)[None],
            (obs_column % lon_cells).astype(f32)[None],
            jnp.zeros((LANES - levels - 4, obs_here), f32),
        ],
        axis=0,
    )
    send = pl.pallas_call(
        pack_kernel,
        out_shape=jax.ShapeDtypeStruct((total, LANES), jnp.bfloat16),
        in_specs=[SMEM, VMEM],
        out_specs=VMEM,
        scratch_shapes=[pltpu.VMEM((obs_here, LANES), f32), pltpu.VMEM((total, LANES), f32)],
        compiler_params=PARAMS,
        name="pack",
    )(obs_slot, payload)
    got = lax.all_to_all(
        send.reshape(devices, slot_count, LANES),
        ("lat", "lon"),
        split_axis=0,
        concat_axis=0,
        tiled=True,
    ).reshape(total, LANES)
    columns = (
        got[:, levels + 2].astype(f32) * lon_cells + got[:, levels + 3].astype(f32)
    ).astype(jnp.int32)

    kappa_ext = extended(kappa, f32)
    kappa_ext = jnp.broadcast_to(kappa_ext[:, :, None], kappa_ext.shape + (LANES,))
    wide = jnp.pad(vertical, ((0, LANES - levels), (0, 0)))
    start = jnp.einsum("kj,jab->abk", wide, control, precision=lax.Precision.HIGHEST)
    start = extended(start, f32)
    ext = start.shape
    state = pl.pallas_call(
        forward_kernel,
        out_shape=jax.ShapeDtypeStruct((lat_rows, lon_cells, LANES), f32),
        in_specs=[VMEM, VMEM],
        out_specs=VMEM,
        scratch_shapes=[pltpu.VMEM(ext, f32), pltpu.VMEM(ext, f32)],
        compiler_params=PARAMS,
        cost_estimate=pl.CostEstimate(flops=40 * start.size, bytes_accessed=12 * start.size, transcendentals=0),
        name="forward",
    )(start, kappa_ext)

    adjoint = pl.pallas_call(
        functools.partial(obs_kernel, levels),
        out_shape=jax.ShapeDtypeStruct((cells, LANES), f32),
        in_specs=[SMEM, VMEM, VMEM],
        out_specs=VMEM,
        scratch_shapes=[pltpu.VMEM((total, LANES), f32)] + [pltpu.VMEM((cells, LANES), f32)] * CHAINS,
        compiler_params=PARAMS,
        name="observe",
    )(columns, got, state.reshape(cells, LANES))

    adjoint = extended(adjoint.reshape(lat_rows, lon_cells, LANES), jnp.bfloat16)
    adjoint = pl.pallas_call(
        adjoint_kernel,
        out_shape=jax.ShapeDtypeStruct((lat_rows, lon_cells, LANES), f32),
        in_specs=[VMEM, VMEM],
        out_specs=VMEM,
        scratch_shapes=[pltpu.VMEM(ext, f32), pltpu.VMEM(ext, f32)],
        compiler_params=PARAMS,
        name="adjoint",
    )(adjoint, kappa_ext)
    back = jnp.einsum("jk,abj->kab", vertical, adjoint[:, :, :levels], precision=lax.Precision.HIGHEST)
    return control + back


def solution(mesh):
    in_specs = (
        P(None, "lat", "lon"),
        P(),
        P("lat", "lon"),
        P(None, ("lat", "lon")),
        P(("lat", "lon")),
        P(("lat", "lon")),
        P(("lat", "lon")),
        P(("lat", "lon")),
    )
    out_specs = P(None, "lat", "lon")
    return jax.shard_map(local, mesh=mesh, in_specs=in_specs, out_specs=out_specs, check_vma=False)
```

```python
import functools

import jax
import jax.numpy as jnp
from jax import lax
from jax.experimental import pallas as pl
from jax.experimental.pallas import tpu as pltpu
from jax.sharding import PartitionSpec as P

NSTEP = 4
LANES = 128
CHAINS = 8
VMEM = pl.BlockSpec(memory_space=pltpu.VMEM)
SMEM = pl.BlockSpec(memory_space=pltpu.SMEM)
PARAMS = pltpu.CompilerParams(vmem_limit_bytes=56 * 2**20)


def pack_kernel(slot_ref, weights_ref, extras_ref, out_ref, rows, slots):
    obs = rows.shape[0]
    rest = LANES - weights_ref.shape[0] - extras_ref.shape[0]

    @pl.loop(0, obs // LANES)
    def _(j):
        at = pl.multiple_of(j * LANES, LANES)
        block = [
            weights_ref[:, pl.ds(at, LANES)].astype(jnp.float32),
            extras_ref[:, pl.ds(at, LANES)],
            jnp.zeros((rest, LANES), jnp.float32),
        ]
        rows[pl.ds(at, LANES), :] = jnp.concatenate(block, axis=0).T

    @pl.loop(0, slots.shape[0] // 256)
    def _(j):
        at = pl.multiple_of(j * 256, 256)
        slots[pl.ds(at, 256), :] = jnp.zeros((256, LANES), jnp.float32)

    @pl.loop(0, obs // 32)
    def _(j):
        at = pl.multiple_of(j * 32, 32)
        for u in range(32):
            slots[pl.ds(slot_ref[at + u], 1), :] = rows[pl.ds(at + u, 1), :]

    @pl.loop(0, slots.shape[0] // 256)
    def _(j):
        at = pl.multiple_of(j * 256, 256)
        out_ref[pl.ds(at, 256), :] = slots[pl.ds(at, 256), :].astype(jnp.bfloat16)


def obs_kernel(levels, col_ref, got_ref, state_ref, out_ref, picked, *sums):
    count = picked.shape[0]
    cells = state_ref.shape[0]

    @pl.loop(0, cells // 256)
    def _(j):
        at = pl.multiple_of(j * 256, 256)
        for s in sums:
            s[pl.ds(at, 256), :] = jnp.zeros((256, LANES), jnp.float32)

    @pl.loop(0, count // 32)
    def _(j):
        at = pl.multiple_of(j * 32, 32)
        for u in range(32):
            picked[pl.ds(at + u, 1), :] = state_ref[pl.ds(col_ref[at + u], 1), :]

    @pl.loop(0, count // 128)
    def _(j):
        at = pl.multiple_of(j * 128, 128)
        w = got_ref[pl.ds(at, 128), :].astype(jnp.float32)
        model = jnp.sum(w * picked[pl.ds(at, 128), :], axis=1, keepdims=True)
        weighted = w[:, levels + 1 : levels + 2] * (model - w[:, levels : levels + 1])
        picked[pl.ds(at, 128), :] = w * weighted

    @pl.loop(0, count // 32)
    def _(j):
        at = pl.multiple_of(j * 32, 32)
        for u in range(0, 32, CHAINS):
            cols = [col_ref[at + u + c] for c in range(CHAINS)]
            old = [sums[c][pl.ds(cols[c], 1), :] for c in range(CHAINS)]
            for c in range(CHAINS):
                sums[c][pl.ds(cols[c], 1), :] = old[c] + picked[pl.ds(at + u + c, 1), :]

    @pl.loop(0, cells // 64)
    def _(j):
        at = pl.multiple_of(j * 64, 64)
        parts = [s[pl.ds(at, 64), :] for s in sums]
        while len(parts) > 1:
            parts = [a + b for a, b in zip(parts[::2], parts[1::2])]
        out_ref[pl.ds(at, 64), :] = parts[0]


def ring(row):
    width = row.shape[0]
    return pltpu.roll(row, 1, 0) + pltpu.roll(row, width - 1, 0)


def forward_kernel(levels, field_ref, out_ref, kappa_ref, one, two):
    rows, lon = out_ref.shape[:2]
    total, width = field_ref.shape[:2]
    kept = lax.broadcasted_iota(jnp.int32, (lon, LANES), 1) < levels

    @pl.loop(0, total)
    def _(r):
        kappa_ref[r] = jnp.broadcast_to(field_ref[r][:, levels : levels + 1], (width, LANES))

    source = field_ref
    for step in range(NSTEP):
        last = step == NSTEP - 1
        target = (one, two)[step % 2]

        @pl.loop(1 + step, total - 1 - step)
        def _(r):
            f = source[r]
            new = f + kappa_ref[r] * (source[r - 1] + source[r + 1] + ring(f) - 4.0 * f)
            if last:
                out_ref[r - NSTEP] = jnp.where(kept, new[:lon], 0.0)
            else:
                target[r] = new

        source = target


def adjoint_kernel(field_ref, kappa_ref, out_ref, z, y):
    rows, lon = out_ref.shape[:2]
    total = field_ref.shape[0]
    source = field_ref
    for step in range(NSTEP):
        last = step == NSTEP - 1

        @pl.loop(step, total - step)
        def _(r):
            y[r] = kappa_ref[r] * source[r]

        @pl.loop(1 + step, total - 1 - step)
        def _(r):
            f = y[r]
            new = source[r] + (y[r - 1] + y[r + 1] + ring(f) - 4.0 * f)
            if last:
                out_ref[r - NSTEP] = new[:lon]
            else:
                z[r] = new

        source = z


def exchange(block, axis, dim, periodic, dtype):
    count = lax.axis_size(axis)
    forward = [(i, i + 1) for i in range(count - 1)]
    if periodic:
        forward.append((count - 1, 0))
    backward = [(target, source) for source, target in forward]
    size = block.shape[dim]
    low = lax.slice_in_dim(block, size - NSTEP, None, axis=dim).astype(dtype)
    high = lax.slice_in_dim(block, 0, NSTEP, axis=dim).astype(dtype)
    low = lax.ppermute(low, axis, forward).astype(block.dtype)
    high = lax.ppermute(high, axis, backward).astype(block.dtype)
    return low, high


def extended(block, dtype):
    low, high = exchange(block, "lon", 1, True, dtype)
    block = jnp.concatenate([block, high, low], axis=1)
    low, high = exchange(block, "lat", 0, False, dtype)
    return jnp.concatenate([low, block, high], axis=0)


def local(control, vertical, kappa, obs_weights, obs_values, obs_precision, obs_slot, obs_column):
    levels, lat_rows, lon_cells = control.shape
    devices = lax.axis_size("lat") * lax.axis_size("lon")
    obs_here = obs_slot.shape[0]
    slot_count = 2 * obs_here // devices
    total = devices * slot_count
    cells = lat_rows * lon_cells
    f32 = jnp.float32

    extras = jnp.stack(
        [
            obs_values.astype(f32),
            obs_precision.astype(f32),
            (obs_column // lon_cells).astype(f32),
            (obs_column % lon_cells).astype(f32),
        ]
        + [jnp.zeros((obs_here,), f32)] * 4
    )
    send = pl.pallas_call(
        pack_kernel,
        out_shape=jax.ShapeDtypeStruct((total, LANES), jnp.bfloat16),
        in_specs=[SMEM, VMEM, VMEM],
        out_specs=VMEM,
        scratch_shapes=[pltpu.VMEM((obs_here, LANES), f32), pltpu.VMEM((total, LANES), f32)],
        compiler_params=PARAMS,
        cost_estimate=pl.CostEstimate(flops=0, bytes_accessed=30 * total * LANES, transcendentals=0),
        name="pack",
    )(obs_slot, obs_weights, extras)
    wide = jnp.pad(vertical, ((0, LANES - levels), (0, 0)))
    start = jnp.einsum("kj,jab->abk", wide, control, precision=lax.Precision.HIGHEST)
    start = start + kappa[:, :, None] * (jnp.arange(LANES) == levels).astype(f32)
    low, high = exchange(start, "lon", 1, True, f32)
    start = jnp.concatenate([start, high, low], axis=1)
    low, high = exchange(start, "lat", 0, False, f32)
    send, low, high = lax.optimization_barrier((send, low, high))
    got = lax.all_to_all(
        send.reshape(devices, slot_count, LANES),
        ("lat", "lon"),
        split_axis=0,
        concat_axis=0,
        tiled=True,
    ).reshape(total, LANES)
    columns = (
        got[:, levels + 2].astype(f32) * lon_cells + got[:, levels + 3].astype(f32)
    ).astype(jnp.int32)
    start = jnp.concatenate([low, start, high], axis=0)
    ext = start.shape
    state, kappa_ext = pl.pallas_call(
        functools.partial(forward_kernel, levels),
        out_shape=(
            jax.ShapeDtypeStruct((lat_rows, lon_cells, LANES), f32),
            jax.ShapeDtypeStruct(ext, f32),
        ),
        in_specs=[VMEM],
        out_specs=(VMEM, VMEM),
        scratch_shapes=[pltpu.VMEM(ext, f32), pltpu.VMEM(ext, f32)],
        compiler_params=PARAMS,
        cost_estimate=pl.CostEstimate(flops=40 * start.size, bytes_accessed=12 * start.size, transcendentals=0),
        name="forward",
    )(start)

    adjoint = pl.pallas_call(
        functools.partial(obs_kernel, levels),
        out_shape=jax.ShapeDtypeStruct((cells, LANES), f32),
        in_specs=[SMEM, VMEM, VMEM],
        out_specs=VMEM,
        scratch_shapes=[pltpu.VMEM((total, LANES), f32)] + [pltpu.VMEM((cells, LANES), f32)] * CHAINS,
        compiler_params=PARAMS,
        name="observe",
    )(columns, got, state.reshape(cells, LANES))

    adjoint = extended(adjoint.reshape(lat_rows, lon_cells, LANES), jnp.bfloat16)
    adjoint = pl.pallas_call(
        adjoint_kernel,
        out_shape=jax.ShapeDtypeStruct((lat_rows, lon_cells, LANES), f32),
        in_specs=[VMEM, VMEM],
        out_specs=VMEM,
        scratch_shapes=[pltpu.VMEM(ext, f32), pltpu.VMEM(ext, f32)],
        compiler_params=PARAMS,
        name="adjoint",
    )(adjoint, kappa_ext)
    back = jnp.einsum("jk,abj->kab", vertical, adjoint[:, :, :levels], precision=lax.Precision.HIGHEST)
    return control + back


def solution(mesh):
    in_specs = (
        P(None, "lat", "lon"),
        P(),
        P("lat", "lon"),
        P(None, ("lat", "lon")),
        P(("lat", "lon")),
        P(("lat", "lon")),
        P(("lat", "lon")),
        P(("lat", "lon")),
    )
    out_specs = P(None, "lat", "lon")
    return jax.shard_map(local, mesh=mesh, in_specs=in_specs, out_specs=out_specs, check_vma=False)
```

```python
import functools

import jax
import jax.numpy as jnp
from jax import lax
from jax.experimental import pallas as pl
from jax.experimental.pallas import tpu as pltpu
from jax.sharding import PartitionSpec as P

NSTEP = 4
LANES = 128
CHAINS = 8
VMEM = pl.BlockSpec(memory_space=pltpu.VMEM)
SMEM = pl.BlockSpec(memory_space=pltpu.SMEM)
PARAMS = pltpu.CompilerParams(vmem_limit_bytes=56 * 2**20)


HEAD = 64


def packing(levels, slot_count):
    tail = levels + 4 - HEAD
    beside = LANES // tail
    return tail, beside, -(-slot_count // (16 * beside)) * 16


def pack_kernel(slot_ref, weights_ref, extras_ref, out_ref, rows, slots):
    obs = rows.shape[0]
    rest = LANES - weights_ref.shape[0] - extras_ref.shape[0]

    @pl.loop(0, obs // LANES)
    def _(j):
        at = pl.multiple_of(j * LANES, LANES)
        block = [
            weights_ref[:, pl.ds(at, LANES)].astype(jnp.float32),
            extras_ref[:, pl.ds(at, LANES)],
            jnp.zeros((rest, LANES), jnp.float32),
        ]
        rows[pl.ds(at, LANES), :] = jnp.concatenate(block, axis=0).T

    @pl.loop(0, slots.shape[0] // 256)
    def _(j):
        at = pl.multiple_of(j * 256, 256)
        slots[pl.ds(at, 256), :] = jnp.zeros((256, LANES), jnp.float32)

    @pl.loop(0, obs // 32)
    def _(j):
        at = pl.multiple_of(j * 32, 32)
        for u in range(32):
            slots[pl.ds(slot_ref[at + u], 1), :] = rows[pl.ds(at + u, 1), :]

    owners = out_ref.shape[0]
    count = slots.shape[0] // owners
    half = count // 2
    tail, beside, group = packing(weights_ref.shape[0], count)
    head_lane = lax.broadcasted_iota(jnp.int32, (half, LANES), 1)
    tail_lane = lax.broadcasted_iota(jnp.int32, (group, LANES), 1)

    @pl.loop(0, owners)
    def _(o):
        at = pl.multiple_of(o * count, count)
        second = pltpu.roll(slots[pl.ds(at + half, half), :], HEAD, 1)
        head = jnp.where(head_lane < HEAD, slots[pl.ds(at, half), :], second)
        out_ref[o, :half, :] = head.astype(jnp.bfloat16)
        tails = jnp.zeros((group, LANES), jnp.float32)
        for g in range(beside):
            size = min(group, count - g * group)
            if size <= 0:
                continue
            rest_rows = slots[pl.ds(at + g * group, size), :]
            if size < group:
                rest_rows = jnp.concatenate([rest_rows, jnp.zeros((group - size, LANES), jnp.float32)], axis=0)
            moved = pltpu.roll(rest_rows, (tail * g - HEAD) % LANES, 1)
            tails = jnp.where((tail_lane >= tail * g) & (tail_lane < tail * (g + 1)), moved, tails)
        out_ref[o, half:, :] = tails.astype(jnp.bfloat16)


def obs_kernel(levels, lon_cells, got_ref, state_ref, out_ref, picked, weights, cols, col_ref, sem, *sums):
    cells = state_ref.shape[0]
    owners, slot_count = cols.shape
    half = slot_count // 2
    tail, beside, group = packing(levels, slot_count)
    unroll = min(slot_count, 32)
    lane = lax.broadcasted_iota(jnp.int32, (8, LANES), 1)
    scale = jnp.where(lane == levels + 2, float(lon_cells), jnp.where(lane == levels + 3, 1.0, 0.0))
    scale = scale.astype(jnp.bfloat16)

    @pl.loop(0, owners)
    def _(o):
        at = pl.multiple_of(o * slot_count, slot_count)
        head = got_ref[o, :half, :].astype(jnp.float32)
        tails = got_ref[o, half:, :].astype(jnp.float32)
        heads = jnp.concatenate([head, pltpu.roll(head, HEAD, 1)], axis=0)
        parts = []
        for g in range(beside):
            size = min(group, slot_count - g * group)
            if size > 0:
                parts.append(pltpu.roll(tails[:size], (HEAD - tail * g) % LANES, 1))
        rest = jnp.concatenate(parts, axis=0)
        which = lax.broadcasted_iota(jnp.int32, (slot_count, LANES), 1)
        rows = jnp.where(which < HEAD, heads, rest)
        weights[pl.ds(at, slot_count), :] = rows
        column = lax.dot_general(
            scale, rows.astype(jnp.bfloat16), (((1,), (1,)), ((), ())), preferred_element_type=jnp.float32
        )
        cols[pl.ds(o, 1), :] = column[:1].astype(jnp.int32)

    copy = pltpu.make_async_copy(cols, col_ref, sem)
    copy.start()

    @pl.loop(0, cells // 256)
    def _(j):
        at = pl.multiple_of(j * 256, 256)
        for s in sums:
            s[pl.ds(at, 256), :] = jnp.zeros((256, LANES), jnp.float32)

    copy.wait()

    @pl.loop(0, owners)
    def _(o):
        @pl.loop(0, slot_count // unroll)
        def _(j):
            at = pl.multiple_of(o * slot_count + j * unroll, unroll)
            for u in range(unroll):
                picked[pl.ds(at + u, 1), :] = state_ref[pl.ds(col_ref[o, j * unroll + u], 1), :]

    @pl.loop(0, owners * slot_count // 128)
    def _(j):
        at = pl.multiple_of(j * 128, 128)
        w = weights[pl.ds(at, 128), :]
        model = jnp.sum(w * picked[pl.ds(at, 128), :], axis=1, keepdims=True)
        weighted = w[:, levels + 1 : levels + 2] * (model - w[:, levels : levels + 1])
        picked[pl.ds(at, 128), :] = w * weighted

    @pl.loop(0, owners)
    def _(o):
        @pl.loop(0, slot_count // unroll)
        def _(j):
            at = pl.multiple_of(o * slot_count + j * unroll, unroll)
            for u in range(0, unroll, CHAINS):
                where = [col_ref[o, j * unroll + u + c] for c in range(CHAINS)]
                old = [sums[c][pl.ds(where[c], 1), :] for c in range(CHAINS)]
                for c in range(CHAINS):
                    sums[c][pl.ds(where[c], 1), :] = old[c] + picked[pl.ds(at + u + c, 1), :]

    @pl.loop(0, cells // 64)
    def _(j):
        at = pl.multiple_of(j * 64, 64)
        parts = [s[pl.ds(at, 64), :] for s in sums]
        while len(parts) > 1:
            parts = [a + b for a, b in zip(parts[::2], parts[1::2])]
        out_ref[pl.ds(at, 64), :] = parts[0]


def ring(row):
    width = row.shape[0]
    return pltpu.roll(row, 1, 0) + pltpu.roll(row, width - 1, 0)


def forward_kernel(levels, field_ref, out_ref, kappa_ref, one, two):
    rows, lon = out_ref.shape[:2]
    total, width = field_ref.shape[:2]
    kept = lax.broadcasted_iota(jnp.int32, (lon, LANES), 1) < levels

    @pl.loop(0, total)
    def _(r):
        kappa_ref[r] = jnp.broadcast_to(field_ref[r][:, levels : levels + 1], (width, LANES))

    source = field_ref
    for step in range(NSTEP):
        last = step == NSTEP - 1
        target = (one, two)[step % 2]

        @pl.loop(1 + step, total - 1 - step)
        def _(r):
            f = source[r]
            new = f + kappa_ref[r] * (source[r - 1] + source[r + 1] + ring(f) - 4.0 * f)
            if last:
                out_ref[r - NSTEP] = jnp.where(kept, new[:lon], 0.0)
            else:
                target[r] = new

        source = target


def adjoint_kernel(field_ref, kappa_ref, out_ref, z, y):
    rows, lon = out_ref.shape[:2]
    total = field_ref.shape[0]
    source = field_ref
    for step in range(NSTEP):
        last = step == NSTEP - 1

        @pl.loop(step, total - step)
        def _(r):
            y[r] = kappa_ref[r] * source[r]

        @pl.loop(1 + step, total - 1 - step)
        def _(r):
            f = y[r]
            new = source[r] + (y[r - 1] + y[r + 1] + ring(f) - 4.0 * f)
            if last:
                out_ref[r - NSTEP] = new[:lon]
            else:
                z[r] = new

        source = z


def exchange(block, axis, dim, periodic, dtype):
    count = lax.axis_size(axis)
    forward = [(i, i + 1) for i in range(count - 1)]
    if periodic:
        forward.append((count - 1, 0))
    backward = [(target, source) for source, target in forward]
    size = block.shape[dim]
    low = lax.slice_in_dim(block, size - NSTEP, None, axis=dim).astype(dtype)
    high = lax.slice_in_dim(block, 0, NSTEP, axis=dim).astype(dtype)
    low = lax.ppermute(low, axis, forward).astype(block.dtype)
    high = lax.ppermute(high, axis, backward).astype(block.dtype)
    return low, high


def extended(block, dtype):
    low, high = exchange(block, "lon", 1, True, dtype)
    block = jnp.concatenate([block, high, low], axis=1)
    low, high = exchange(block, "lat", 0, False, dtype)
    return jnp.concatenate([low, block, high], axis=0)


def local(control, vertical, kappa, obs_weights, obs_values, obs_precision, obs_slot, obs_column):
    levels, lat_rows, lon_cells = control.shape
    devices = lax.axis_size("lat") * lax.axis_size("lon")
    obs_here = obs_slot.shape[0]
    slot_count = 2 * obs_here // devices
    total = devices * slot_count
    cells = lat_rows * lon_cells
    f32 = jnp.float32

    extras = jnp.stack(
        [
            obs_values.astype(f32),
            obs_precision.astype(f32),
            (obs_column // lon_cells).astype(f32),
            (obs_column % lon_cells).astype(f32),
        ]
        + [jnp.zeros((obs_here,), f32)] * 4
    )
    packed = slot_count // 2 + packing(levels, slot_count)[2]
    send = pl.pallas_call(
        pack_kernel,
        out_shape=jax.ShapeDtypeStruct((devices, packed, LANES), jnp.bfloat16),
        in_specs=[SMEM, VMEM, VMEM],
        out_specs=VMEM,
        scratch_shapes=[pltpu.VMEM((obs_here, LANES), f32), pltpu.VMEM((total, LANES), f32)],
        compiler_params=PARAMS,
        cost_estimate=pl.CostEstimate(flops=0, bytes_accessed=30 * total * LANES, transcendentals=0),
        name="pack",
    )(obs_slot, obs_weights, extras)
    wide = jnp.pad(vertical, ((0, LANES - levels), (0, 0)))
    start = jnp.einsum("kj,jab->abk", wide, control, precision=lax.Precision.HIGHEST)
    start = start + kappa[:, :, None] * (jnp.arange(LANES) == levels).astype(f32)
    low, high = exchange(start, "lon", 1, True, f32)
    start = jnp.concatenate([start, high, low], axis=1)
    low, high = exchange(start, "lat", 0, False, f32)
    send, low, high = lax.optimization_barrier((send, low, high))
    got = lax.all_to_all(send, ("lat", "lon"), split_axis=0, concat_axis=0, tiled=True)
    start = jnp.concatenate([low, start, high], axis=0)
    ext = start.shape
    state, kappa_ext = pl.pallas_call(
        functools.partial(forward_kernel, levels),
        out_shape=(
            jax.ShapeDtypeStruct((lat_rows, lon_cells, LANES), f32),
            jax.ShapeDtypeStruct(ext, f32),
        ),
        in_specs=[VMEM],
        out_specs=(VMEM, VMEM),
        scratch_shapes=[pltpu.VMEM(ext, f32), pltpu.VMEM(ext, f32)],
        compiler_params=PARAMS,
        cost_estimate=pl.CostEstimate(flops=40 * start.size, bytes_accessed=12 * start.size, transcendentals=0),
        name="forward",
    )(start)

    adjoint = pl.pallas_call(
        functools.partial(obs_kernel, levels, lon_cells),
        out_shape=jax.ShapeDtypeStruct((cells, LANES), f32),
        in_specs=[VMEM, VMEM],
        out_specs=VMEM,
        scratch_shapes=[
            pltpu.VMEM((total, LANES), f32),
            pltpu.VMEM((total, LANES), f32),
            pltpu.VMEM((devices, slot_count), jnp.int32),
            pltpu.SMEM((devices, slot_count), jnp.int32),
            pltpu.SemaphoreType.DMA,
        ]
        + [pltpu.VMEM((cells, LANES), f32)] * CHAINS,
        compiler_params=PARAMS,
        name="observe",
    )(got, state.reshape(cells, LANES))

    adjoint = extended(adjoint.reshape(lat_rows, lon_cells, LANES), jnp.bfloat16)
    adjoint = pl.pallas_call(
        adjoint_kernel,
        out_shape=jax.ShapeDtypeStruct((lat_rows, lon_cells, LANES), f32),
        in_specs=[VMEM, VMEM],
        out_specs=VMEM,
        scratch_shapes=[pltpu.VMEM(ext, f32), pltpu.VMEM(ext, f32)],
        compiler_params=PARAMS,
        name="adjoint",
    )(adjoint, kappa_ext)
    back = jnp.einsum("jk,abj->kab", vertical, adjoint[:, :, :levels], precision=lax.Precision.HIGHEST)
    return control + back


def solution(mesh):
    in_specs = (
        P(None, "lat", "lon"),
        P(),
        P("lat", "lon"),
        P(None, ("lat", "lon")),
        P(("lat", "lon")),
        P(("lat", "lon")),
        P(("lat", "lon")),
        P(("lat", "lon")),
    )
    out_specs = P(None, "lat", "lon")
    return jax.shard_map(local, mesh=mesh, in_specs=in_specs, out_specs=out_specs, check_vma=False)
```

```python
import functools

import jax
import jax.numpy as jnp
from jax import lax
from jax.experimental import pallas as pl
from jax.experimental.pallas import tpu as pltpu
from jax.sharding import PartitionSpec as P

NSTEP = 4
LANES = 128
CHAINS = 8
VMEM = pl.BlockSpec(memory_space=pltpu.VMEM)
SMEM = pl.BlockSpec(memory_space=pltpu.SMEM)
PARAMS = pltpu.CompilerParams(vmem_limit_bytes=56 * 2**20)


HEAD = 64


def packing(levels, slot_count):
    tail = levels + 4 - HEAD
    beside = LANES // tail
    return tail, beside, -(-slot_count // (16 * beside)) * 16


def pack_kernel(slot_ref, weights_ref, extras_ref, out_ref, rows, slots):
    obs = rows.shape[0]
    rest = LANES - weights_ref.shape[0] - extras_ref.shape[0]

    @pl.loop(0, obs // LANES)
    def _(j):
        at = pl.multiple_of(j * LANES, LANES)
        block = [
            weights_ref[:, pl.ds(at, LANES)].astype(jnp.float32),
            extras_ref[:, pl.ds(at, LANES)],
            jnp.zeros((rest, LANES), jnp.float32),
        ]
        rows[pl.ds(at, LANES), :] = jnp.concatenate(block, axis=0).T

    @pl.loop(0, slots.shape[0] // 256)
    def _(j):
        at = pl.multiple_of(j * 256, 256)
        slots[pl.ds(at, 256), :] = jnp.zeros((256, LANES), jnp.float32)

    @pl.loop(0, obs // 32)
    def _(j):
        at = pl.multiple_of(j * 32, 32)
        for u in range(32):
            slots[pl.ds(slot_ref[at + u], 1), :] = rows[pl.ds(at + u, 1), :]

    owners = out_ref.shape[0]
    count = slots.shape[0] // owners
    half = count // 2
    tail, beside, group = packing(weights_ref.shape[0], count)
    head_lane = lax.broadcasted_iota(jnp.int32, (half, LANES), 1)
    tail_lane = lax.broadcasted_iota(jnp.int32, (group, LANES), 1)

    @pl.loop(0, owners)
    def _(o):
        at = pl.multiple_of(o * count, count)
        second = pltpu.roll(slots[pl.ds(at + half, half), :], HEAD, 1)
        head = jnp.where(head_lane < HEAD, slots[pl.ds(at, half), :], second)
        out_ref[o, :half, :] = head.astype(jnp.bfloat16)
        tails = jnp.zeros((group, LANES), jnp.float32)
        for g in range(beside):
            size = min(group, count - g * group)
            if size <= 0:
                continue
            rest_rows = slots[pl.ds(at + g * group, size), :]
            if size < group:
                rest_rows = jnp.concatenate([rest_rows, jnp.zeros((group - size, LANES), jnp.float32)], axis=0)
            moved = pltpu.roll(rest_rows, (tail * g - HEAD) % LANES, 1)
            tails = jnp.where((tail_lane >= tail * g) & (tail_lane < tail * (g + 1)), moved, tails)
        out_ref[o, half:, :] = tails.astype(jnp.bfloat16)


def unpack_kernel(levels, lon_cells, got_ref, weights, cols):
    owners, slot_count = cols.shape
    half = slot_count // 2
    tail, beside, group = packing(levels, slot_count)
    lane = lax.broadcasted_iota(jnp.int32, (8, LANES), 1)
    scale = jnp.where(lane == levels + 2, float(lon_cells), jnp.where(lane == levels + 3, 1.0, 0.0))
    scale = scale.astype(jnp.bfloat16)

    @pl.loop(0, owners)
    def _(o):
        at = pl.multiple_of(o * slot_count, slot_count)
        head = got_ref[o, :half, :].astype(jnp.float32)
        tails = got_ref[o, half:, :].astype(jnp.float32)
        heads = jnp.concatenate([head, pltpu.roll(head, HEAD, 1)], axis=0)
        parts = []
        for g in range(beside):
            size = min(group, slot_count - g * group)
            if size > 0:
                parts.append(pltpu.roll(tails[:size], (HEAD - tail * g) % LANES, 1))
        rest = jnp.concatenate(parts, axis=0)
        which = lax.broadcasted_iota(jnp.int32, (slot_count, LANES), 1)
        rows = jnp.where(which < HEAD, heads, rest)
        weights[pl.ds(at, slot_count), :] = rows
        column = lax.dot_general(
            scale, rows.astype(jnp.bfloat16), (((1,), (1,)), ((), ())), preferred_element_type=jnp.float32
        )
        cols[pl.ds(o, 1), :] = column[:1].astype(jnp.int32)


def obs_kernel(levels, col_ref, got_ref, state_ref, out_ref, picked, *sums):
    count = picked.shape[0]
    cells = state_ref.shape[0]

    @pl.loop(0, cells // 256)
    def _(j):
        at = pl.multiple_of(j * 256, 256)
        for s in sums:
            s[pl.ds(at, 256), :] = jnp.zeros((256, LANES), jnp.float32)

    @pl.loop(0, count // 32)
    def _(j):
        at = pl.multiple_of(j * 32, 32)
        for u in range(32):
            picked[pl.ds(at + u, 1), :] = state_ref[pl.ds(col_ref[at + u], 1), :]

    @pl.loop(0, count // 128)
    def _(j):
        at = pl.multiple_of(j * 128, 128)
        w = got_ref[pl.ds(at, 128), :].astype(jnp.float32)
        model = jnp.sum(w * picked[pl.ds(at, 128), :], axis=1, keepdims=True)
        weighted = w[:, levels + 1 : levels + 2] * (model - w[:, levels : levels + 1])
        picked[pl.ds(at, 128), :] = w * weighted

    @pl.loop(0, count // 32)
    def _(j):
        at = pl.multiple_of(j * 32, 32)
        for u in range(0, 32, CHAINS):
            cols = [col_ref[at + u + c] for c in range(CHAINS)]
            old = [sums[c][pl.ds(cols[c], 1), :] for c in range(CHAINS)]
            for c in range(CHAINS):
                sums[c][pl.ds(cols[c], 1), :] = old[c] + picked[pl.ds(at + u + c, 1), :]

    @pl.loop(0, cells // 64)
    def _(j):
        at = pl.multiple_of(j * 64, 64)
        parts = [s[pl.ds(at, 64), :] for s in sums]
        while len(parts) > 1:
            parts = [a + b for a, b in zip(parts[::2], parts[1::2])]
        out_ref[pl.ds(at, 64), :] = parts[0]


def ring(row):
    width = row.shape[0]
    return pltpu.roll(row, 1, 0) + pltpu.roll(row, width - 1, 0)


def forward_kernel(levels, field_ref, out_ref, kappa_ref, one, two):
    rows, lon = out_ref.shape[:2]
    total, width = field_ref.shape[:2]
    kept = lax.broadcasted_iota(jnp.int32, (lon, LANES), 1) < levels

    @pl.loop(0, total)
    def _(r):
        kappa_ref[r] = jnp.broadcast_to(field_ref[r][:, levels : levels + 1], (width, LANES))

    source = field_ref
    for step in range(NSTEP):
        last = step == NSTEP - 1
        target = (one, two)[step % 2]

        @pl.loop(1 + step, total - 1 - step)
        def _(r):
            f = source[r]
            new = f + kappa_ref[r] * (source[r - 1] + source[r + 1] + ring(f) - 4.0 * f)
            if last:
                out_ref[r - NSTEP] = jnp.where(kept, new[:lon], 0.0)
            else:
                target[r] = new

        source = target


def adjoint_kernel(field_ref, kappa_ref, out_ref, z, y):
    rows, lon = out_ref.shape[:2]
    total = field_ref.shape[0]
    source = field_ref
    for step in range(NSTEP):
        last = step == NSTEP - 1

        @pl.loop(step, total - step)
        def _(r):
            y[r] = kappa_ref[r] * source[r]

        @pl.loop(1 + step, total - 1 - step)
        def _(r):
            f = y[r]
            new = source[r] + (y[r - 1] + y[r + 1] + ring(f) - 4.0 * f)
            if last:
                out_ref[r - NSTEP] = new[:lon]
            else:
                z[r] = new

        source = z


def exchange(block, axis, dim, periodic, dtype):
    count = lax.axis_size(axis)
    forward = [(i, i + 1) for i in range(count - 1)]
    if periodic:
        forward.append((count - 1, 0))
    backward = [(target, source) for source, target in forward]
    size = block.shape[dim]
    low = lax.slice_in_dim(block, size - NSTEP, None, axis=dim).astype(dtype)
    high = lax.slice_in_dim(block, 0, NSTEP, axis=dim).astype(dtype)
    low = lax.ppermute(low, axis, forward).astype(block.dtype)
    high = lax.ppermute(high, axis, backward).astype(block.dtype)
    return low, high


def extended(block, dtype):
    low, high = exchange(block, "lon", 1, True, dtype)
    block = jnp.concatenate([block, high, low], axis=1)
    low, high = exchange(block, "lat", 0, False, dtype)
    return jnp.concatenate([low, block, high], axis=0)


def local(control, vertical, kappa, obs_weights, obs_values, obs_precision, obs_slot, obs_column):
    levels, lat_rows, lon_cells = control.shape
    devices = lax.axis_size("lat") * lax.axis_size("lon")
    obs_here = obs_slot.shape[0]
    slot_count = 2 * obs_here // devices
    total = devices * slot_count
    cells = lat_rows * lon_cells
    f32 = jnp.float32

    extras = jnp.stack(
        [
            obs_values.astype(f32),
            obs_precision.astype(f32),
            (obs_column // lon_cells).astype(f32),
            (obs_column % lon_cells).astype(f32),
        ]
        + [jnp.zeros((obs_here,), f32)] * 4
    )
    packed = slot_count // 2 + packing(levels, slot_count)[2]
    send = pl.pallas_call(
        pack_kernel,
        out_shape=jax.ShapeDtypeStruct((devices, packed, LANES), jnp.bfloat16),
        in_specs=[SMEM, VMEM, VMEM],
        out_specs=VMEM,
        scratch_shapes=[pltpu.VMEM((obs_here, LANES), f32), pltpu.VMEM((total, LANES), f32)],
        compiler_params=PARAMS,
        cost_estimate=pl.CostEstimate(flops=0, bytes_accessed=30 * total * LANES, transcendentals=0),
        name="pack",
    )(obs_slot, obs_weights, extras)
    wide = jnp.pad(vertical, ((0, LANES - levels), (0, 0)))
    start = jnp.einsum("kj,jab->abk", wide, control, precision=lax.Precision.HIGHEST)
    start = start + kappa[:, :, None] * (jnp.arange(LANES) == levels).astype(f32)
    low, high = exchange(start, "lon", 1, True, f32)
    start = jnp.concatenate([start, high, low], axis=1)
    low, high = exchange(start, "lat", 0, False, f32)
    send, low, high = lax.optimization_barrier((send, low, high))
    got = lax.all_to_all(send, ("lat", "lon"), split_axis=0, concat_axis=0, tiled=True)
    start = jnp.concatenate([low, start, high], axis=0)
    ext = start.shape
    state, kappa_ext = pl.pallas_call(
        functools.partial(forward_kernel, levels),
        out_shape=(
            jax.ShapeDtypeStruct((lat_rows, lon_cells, LANES), f32),
            jax.ShapeDtypeStruct(ext, f32),
        ),
        in_specs=[VMEM],
        out_specs=(VMEM, VMEM),
        scratch_shapes=[pltpu.VMEM(ext, f32), pltpu.VMEM(ext, f32)],
        compiler_params=PARAMS,
        cost_estimate=pl.CostEstimate(flops=40 * start.size, bytes_accessed=12 * start.size, transcendentals=0),
        name="forward",
    )(start)

    got, columns = pl.pallas_call(
        functools.partial(unpack_kernel, levels, lon_cells),
        out_shape=(
            jax.ShapeDtypeStruct((total, LANES), f32),
            jax.ShapeDtypeStruct((devices, slot_count), jnp.int32),
        ),
        in_specs=[VMEM],
        out_specs=(VMEM, VMEM),
        compiler_params=PARAMS,
        name="unpack",
    )(got)
    adjoint = pl.pallas_call(
        functools.partial(obs_kernel, levels),
        out_shape=jax.ShapeDtypeStruct((cells, LANES), f32),
        in_specs=[SMEM, VMEM, VMEM],
        out_specs=VMEM,
        scratch_shapes=[pltpu.VMEM((total, LANES), f32)] + [pltpu.VMEM((cells, LANES), f32)] * CHAINS,
        compiler_params=PARAMS,
        name="observe",
    )(columns.reshape(total), got, state.reshape(cells, LANES))

    adjoint = extended(adjoint.reshape(lat_rows, lon_cells, LANES), jnp.bfloat16)
    adjoint = pl.pallas_call(
        adjoint_kernel,
        out_shape=jax.ShapeDtypeStruct((lat_rows, lon_cells, LANES), f32),
        in_specs=[VMEM, VMEM],
        out_specs=VMEM,
        scratch_shapes=[pltpu.VMEM(ext, f32), pltpu.VMEM(ext, f32)],
        compiler_params=PARAMS,
        name="adjoint",
    )(adjoint, kappa_ext)
    back = jnp.einsum("jk,abj->kab", vertical, adjoint[:, :, :levels], precision=lax.Precision.HIGHEST)
    return control + back


def solution(mesh):
    in_specs = (
        P(None, "lat", "lon"),
        P(),
        P("lat", "lon"),
        P(None, ("lat", "lon")),
        P(("lat", "lon")),
        P(("lat", "lon")),
        P(("lat", "lon")),
        P(("lat", "lon")),
    )
    out_specs = P(None, "lat", "lon")
    return jax.shard_map(local, mesh=mesh, in_specs=in_specs, out_specs=out_specs, check_vma=False)
```

```python
import functools

import jax
import jax.numpy as jnp
from jax import lax
from jax.experimental import pallas as pl
from jax.experimental.pallas import tpu as pltpu
from jax.sharding import PartitionSpec as P

NSTEP = 4
LANES = 128
CHAINS = 8
VMEM = pl.BlockSpec(memory_space=pltpu.VMEM)
SMEM = pl.BlockSpec(memory_space=pltpu.SMEM)
PARAMS = pltpu.CompilerParams(vmem_limit_bytes=56 * 2**20)


HEAD = 64


def packing(levels, slot_count):
    tail = levels + 4 - HEAD
    beside = LANES // tail
    return tail, beside, -(-slot_count // (16 * beside)) * 16


def pack_kernel(slot_ref, weights_ref, extras_ref, out_ref, rows, slots):
    obs = rows.shape[0]
    rest = LANES - weights_ref.shape[0] - extras_ref.shape[0]

    @pl.loop(0, obs // LANES, unroll=4)
    def _(j):
        at = pl.multiple_of(j * LANES, LANES)
        block = [
            weights_ref[:, pl.ds(at, LANES)].astype(jnp.float32),
            extras_ref[:, pl.ds(at, LANES)],
            jnp.zeros((rest, LANES), jnp.float32),
        ]
        rows[pl.ds(at, LANES), :] = jnp.concatenate(block, axis=0).T

    @pl.loop(0, slots.shape[0] // 256)
    def _(j):
        at = pl.multiple_of(j * 256, 256)
        slots[pl.ds(at, 256), :] = jnp.zeros((256, LANES), jnp.float32)

    @pl.loop(0, obs // 32)
    def _(j):
        at = pl.multiple_of(j * 32, 32)
        for u in range(32):
            slots[pl.ds(slot_ref[at + u], 1), :] = rows[pl.ds(at + u, 1), :]

    owners = out_ref.shape[0]
    count = slots.shape[0] // owners
    half = count // 2
    tail, beside, group = packing(weights_ref.shape[0], count)
    head_lane = lax.broadcasted_iota(jnp.int32, (half, LANES), 1)
    tail_lane = lax.broadcasted_iota(jnp.int32, (group, LANES), 1)

    @pl.loop(0, owners, unroll=4)
    def _(o):
        at = pl.multiple_of(o * count, count)
        second = pltpu.roll(slots[pl.ds(at + half, half), :], HEAD, 1)
        head = jnp.where(head_lane < HEAD, slots[pl.ds(at, half), :], second)
        out_ref[o, :half, :] = head.astype(jnp.bfloat16)
        tails = jnp.zeros((group, LANES), jnp.float32)
        for g in range(beside):
            size = min(group, count - g * group)
            if size <= 0:
                continue
            rest_rows = slots[pl.ds(at + g * group, size), :]
            if size < group:
                rest_rows = jnp.concatenate([rest_rows, jnp.zeros((group - size, LANES), jnp.float32)], axis=0)
            moved = pltpu.roll(rest_rows, (tail * g - HEAD) % LANES, 1)
            tails = jnp.where((tail_lane >= tail * g) & (tail_lane < tail * (g + 1)), moved, tails)
        out_ref[o, half:, :] = tails.astype(jnp.bfloat16)


def unpack_kernel(levels, lon_cells, got_ref, weights, cols):
    owners, slot_count = cols.shape
    half = slot_count // 2
    tail, beside, group = packing(levels, slot_count)
    lane = lax.broadcasted_iota(jnp.int32, (8, LANES), 1)
    scale = jnp.where(lane == levels + 2, float(lon_cells), jnp.where(lane == levels + 3, 1.0, 0.0))
    scale = scale.astype(jnp.bfloat16)

    @pl.loop(0, owners, unroll=4)
    def _(o):
        at = pl.multiple_of(o * slot_count, slot_count)
        head = got_ref[o, :half, :].astype(jnp.float32)
        tails = got_ref[o, half:, :].astype(jnp.float32)
        heads = jnp.concatenate([head, pltpu.roll(head, HEAD, 1)], axis=0)
        parts = []
        for g in range(beside):
            size = min(group, slot_count - g * group)
            if size > 0:
                parts.append(pltpu.roll(tails[:size], (HEAD - tail * g) % LANES, 1))
        rest = jnp.concatenate(parts, axis=0)
        which = lax.broadcasted_iota(jnp.int32, (slot_count, LANES), 1)
        rows = jnp.where(which < HEAD, heads, rest)
        weights[pl.ds(at, slot_count), :] = rows
        column = lax.dot_general(
            scale, rows.astype(jnp.bfloat16), (((1,), (1,)), ((), ())), preferred_element_type=jnp.float32
        )
        cols[pl.ds(o, 1), :] = column[:1].astype(jnp.int32)


def obs_kernel(levels, col_ref, got_ref, state_ref, out_ref, picked, *sums):
    count = picked.shape[0]
    cells = state_ref.shape[0]

    @pl.loop(0, cells // 256)
    def _(j):
        at = pl.multiple_of(j * 256, 256)
        for s in sums:
            s[pl.ds(at, 256), :] = jnp.zeros((256, LANES), jnp.float32)

    @pl.loop(0, count // 32)
    def _(j):
        at = pl.multiple_of(j * 32, 32)
        for u in range(32):
            picked[pl.ds(at + u, 1), :] = state_ref[pl.ds(col_ref[at + u], 1), :]

    @pl.loop(0, count // 128, unroll=4)
    def _(j):
        at = pl.multiple_of(j * 128, 128)
        w = got_ref[pl.ds(at, 128), :].astype(jnp.float32)
        model = jnp.sum(w * picked[pl.ds(at, 128), :], axis=1, keepdims=True)
        weighted = w[:, levels + 1 : levels + 2] * (model - w[:, levels : levels + 1])
        picked[pl.ds(at, 128), :] = w * weighted

    @pl.loop(0, count // 32)
    def _(j):
        at = pl.multiple_of(j * 32, 32)
        for u in range(0, 32, CHAINS):
            cols = [col_ref[at + u + c] for c in range(CHAINS)]
            old = [sums[c][pl.ds(cols[c], 1), :] for c in range(CHAINS)]
            for c in range(CHAINS):
                sums[c][pl.ds(cols[c], 1), :] = old[c] + picked[pl.ds(at + u + c, 1), :]

    @pl.loop(0, cells // 64)
    def _(j):
        at = pl.multiple_of(j * 64, 64)
        parts = [s[pl.ds(at, 64), :] for s in sums]
        while len(parts) > 1:
            parts = [a + b for a, b in zip(parts[::2], parts[1::2])]
        out_ref[pl.ds(at, 64), :] = parts[0]


def ring(row):
    width = row.shape[0]
    return pltpu.roll(row, 1, 0) + pltpu.roll(row, width - 1, 0)


def forward_kernel(levels, field_ref, out_ref, kappa_ref, one, two):
    rows, lon = out_ref.shape[:2]
    total, width = field_ref.shape[:2]
    kept = lax.broadcasted_iota(jnp.int32, (lon, LANES), 1) < levels

    @pl.loop(0, total)
    def _(r):
        kappa_ref[r] = jnp.broadcast_to(field_ref[r][:, levels : levels + 1], (width, LANES))

    source = field_ref
    for step in range(NSTEP):
        last = step == NSTEP - 1
        target = (one, two)[step % 2]

        @pl.loop(1 + step, total - 1 - step)
        def _(r):
            f = source[r]
            new = f + kappa_ref[r] * (source[r - 1] + source[r + 1] + ring(f) - 4.0 * f)
            if last:
                out_ref[r - NSTEP] = jnp.where(kept, new[:lon], 0.0)
            else:
                target[r] = new

        source = target


def adjoint_kernel(field_ref, kappa_ref, out_ref, z, y):
    rows, lon = out_ref.shape[:2]
    total = field_ref.shape[0]
    source = field_ref
    for step in range(NSTEP):
        last = step == NSTEP - 1

        @pl.loop(step, total - step)
        def _(r):
            y[r] = kappa_ref[r] * source[r]

        @pl.loop(1 + step, total - 1 - step)
        def _(r):
            f = y[r]
            new = source[r] + (y[r - 1] + y[r + 1] + ring(f) - 4.0 * f)
            if last:
                out_ref[r - NSTEP] = new[:lon]
            else:
                z[r] = new

        source = z


def exchange(block, axis, dim, periodic, dtype):
    count = lax.axis_size(axis)
    forward = [(i, i + 1) for i in range(count - 1)]
    if periodic:
        forward.append((count - 1, 0))
    backward = [(target, source) for source, target in forward]
    size = block.shape[dim]
    low = lax.slice_in_dim(block, size - NSTEP, None, axis=dim).astype(dtype)
    high = lax.slice_in_dim(block, 0, NSTEP, axis=dim).astype(dtype)
    low = lax.ppermute(low, axis, forward).astype(block.dtype)
    high = lax.ppermute(high, axis, backward).astype(block.dtype)
    return low, high


def extended(block, dtype):
    low, high = exchange(block, "lon", 1, True, dtype)
    block = jnp.concatenate([block, high, low], axis=1)
    low, high = exchange(block, "lat", 0, False, dtype)
    return jnp.concatenate([low, block, high], axis=0)


def local(control, vertical, kappa, obs_weights, obs_values, obs_precision, obs_slot, obs_column):
    levels, lat_rows, lon_cells = control.shape
    devices = lax.axis_size("lat") * lax.axis_size("lon")
    obs_here = obs_slot.shape[0]
    slot_count = 2 * obs_here // devices
    total = devices * slot_count
    cells = lat_rows * lon_cells
    f32 = jnp.float32

    extras = jnp.stack(
        [
            obs_values.astype(f32),
            obs_precision.astype(f32),
            (obs_column // lon_cells).astype(f32),
            (obs_column % lon_cells).astype(f32),
        ]
        + [jnp.zeros((obs_here,), f32)] * 4
    )
    packed = slot_count // 2 + packing(levels, slot_count)[2]
    send = pl.pallas_call(
        pack_kernel,
        out_shape=jax.ShapeDtypeStruct((devices, packed, LANES), jnp.bfloat16),
        in_specs=[SMEM, VMEM, VMEM],
        out_specs=VMEM,
        scratch_shapes=[pltpu.VMEM((obs_here, LANES), f32), pltpu.VMEM((total, LANES), f32)],
        compiler_params=PARAMS,
        cost_estimate=pl.CostEstimate(flops=0, bytes_accessed=30 * total * LANES, transcendentals=0),
        name="pack",
    )(obs_slot, obs_weights, extras)
    wide = jnp.pad(vertical, ((0, LANES - levels), (0, 0)))
    start = jnp.einsum("kj,jab->abk", wide, control, precision=lax.Precision.HIGHEST)
    start = start + kappa[:, :, None] * (jnp.arange(LANES) == levels).astype(f32)
    low, high = exchange(start, "lon", 1, True, f32)
    start = jnp.concatenate([start, high, low], axis=1)
    low, high = exchange(start, "lat", 0, False, f32)
    send, low, high = lax.optimization_barrier((send, low, high))
    got = lax.all_to_all(send, ("lat", "lon"), split_axis=0, concat_axis=0, tiled=True)
    start = jnp.concatenate([low, start, high], axis=0)
    ext = start.shape
    state, kappa_ext = pl.pallas_call(
        functools.partial(forward_kernel, levels),
        out_shape=(
            jax.ShapeDtypeStruct((lat_rows, lon_cells, LANES), f32),
            jax.ShapeDtypeStruct(ext, f32),
        ),
        in_specs=[VMEM],
        out_specs=(VMEM, VMEM),
        scratch_shapes=[pltpu.VMEM(ext, f32), pltpu.VMEM(ext, f32)],
        compiler_params=PARAMS,
        cost_estimate=pl.CostEstimate(flops=40 * start.size, bytes_accessed=12 * start.size, transcendentals=0),
        name="forward",
    )(start)

    got, columns = pl.pallas_call(
        functools.partial(unpack_kernel, levels, lon_cells),
        out_shape=(
            jax.ShapeDtypeStruct((total, LANES), f32),
            jax.ShapeDtypeStruct((devices, slot_count), jnp.int32),
        ),
        in_specs=[VMEM],
        out_specs=(VMEM, VMEM),
        compiler_params=PARAMS,
        name="unpack",
    )(got)
    adjoint = pl.pallas_call(
        functools.partial(obs_kernel, levels),
        out_shape=jax.ShapeDtypeStruct((cells, LANES), f32),
        in_specs=[SMEM, VMEM, VMEM],
        out_specs=VMEM,
        scratch_shapes=[pltpu.VMEM((total, LANES), f32)] + [pltpu.VMEM((cells, LANES), f32)] * CHAINS,
        compiler_params=PARAMS,
        name="observe",
    )(columns.reshape(total), got, state.reshape(cells, LANES))

    adjoint = extended(adjoint.reshape(lat_rows, lon_cells, LANES), jnp.bfloat16)
    adjoint = pl.pallas_call(
        adjoint_kernel,
        out_shape=jax.ShapeDtypeStruct((lat_rows, lon_cells, LANES), f32),
        in_specs=[VMEM, VMEM],
        out_specs=VMEM,
        scratch_shapes=[pltpu.VMEM(ext, f32), pltpu.VMEM(ext, f32)],
        compiler_params=PARAMS,
        name="adjoint",
    )(adjoint, kappa_ext)
    back = jnp.einsum("jk,abj->kab", vertical, adjoint[:, :, :levels], precision=lax.Precision.HIGHEST)
    return control + back


def solution(mesh):
    in_specs = (
        P(None, "lat", "lon"),
        P(),
        P("lat", "lon"),
        P(None, ("lat", "lon")),
        P(("lat", "lon")),
        P(("lat", "lon")),
        P(("lat", "lon")),
        P(("lat", "lon")),
    )
    out_specs = P(None, "lat", "lon")
    return jax.shard_map(local, mesh=mesh, in_specs=in_specs, out_specs=out_specs, check_vma=False)
```
